256 devices in a mesh: ctx: 32 (over y, x, core), head: 8 (over z).
Axes of the slice: x: 4, y: 4, z: 8, core: 2. Of those that a mesh axis runs over, the one named last changes fastest.
Arguments:
- queries: bfloat16 [32768, 4096], P(('ctx', 'head')), may hold values from -8 to 8
- key_vectors: bfloat16 [32768, 4096], P(('ctx', 'head')), may hold values from -8 to 8
- value_vectors: bfloat16 [32768, 4096], P(('ctx', 'head')), may hold values from -6 to 6
- out_grad: bfloat16 [32768, 4096], P(('ctx', 'head')), may hold values from -6 to 6
- doc_ids: int32 [256], P('ctx'), may hold values from 0 to 15, as said below
Outputs:
- attended: bfloat16 [32768, 4096], P(('ctx', 'head'))
- query_grad: bfloat16 [32768, 4096], P(('ctx', 'head'))
- key_grad: bfloat16 [32768, 4096], P(('ctx', 'head'))
- value_grad: bfloat16 [32768, 4096], P(('ctx', 'head'))
The draws below stay inside these ranges and needn't reach their ends.
Inputs may be any that keep to these rules, and one draw needn't show every extreme that they name: `doc_ids`: document numbers never fall along the stretches and every number is used. Document 0 has exactly 96 stretches, no document has more, and the last document has more than 8 stretches.
All inputs are finite; a program needn't handle non-finite values.
Results may differ from the reference program's by a relative error of at most 0.0095.
Values may be sent and summed in bfloat16 or wider, within the bound.
A program may use at most 128 MiB of HBM per device.

```python
from functools import partial
import jax
import jax.numpy as jnp
from jax import lax

HEADS = 32
HD = 128
STRETCH = 128
TOK_DEV = 1024
TOKENS = 32768
NCHUNK = 256
DOCS = 16
DOC_MOST = 96


def draw_doc_ids(key, part):
    key = jax.random.fold_in(key, 11)
    per_device = TOK_DEV // STRETCH
    middle = DOCS - 2
    remaining = NCHUNK - DOC_MOST
    spread = max(1, min(per_device // 2, (remaining - middle * per_device - per_device - 1) // middle))
    extras = jax.random.randint(key, (middle,), 0, spread + 1).astype(jnp.int32)
    lengths = per_device + extras
    bounds = DOC_MOST + jnp.cumsum(lengths).astype(jnp.int32)
    starts = jnp.concatenate([jnp.array([DOC_MOST], jnp.int32), bounds]).astype(jnp.int32)
    positions = jnp.arange(NCHUNK).astype(jnp.int32)
    return jnp.sum((positions[:, None] >= starts[None, :]).astype(jnp.int32), axis=1).astype(jnp.int32)


def block_scale(stream_key, dims, pieces, smallest, largest):
    gain = 1.0
    for axis_at, shards_of in pieces:
        heights = jax.random.uniform(jax.random.fold_in(jax.random.fold_in(stream_key, 6), axis_at), (shards_of,), jnp.float32, smallest / len(pieces), largest / len(pieces))
        gain = gain * jnp.repeat(jnp.exp(heights), dims[axis_at] // shards_of).reshape((-1,) + (1,) * (len(dims) - 1 - axis_at))
    return gain


def scatter_about(rng, dims, scale, bound, shards=(), kind=jnp.bfloat16):
    values = scale * jax.random.normal(rng, dims, jnp.float32)
    if shards:
        values = values * block_scale(rng, dims, shards, -0.22, 0.18)
    return jnp.clip(values, -bound, bound).astype(kind)


def setup_inputs(seed: int = 0) -> dict:
    streams_of = jax.random.split(jax.random.key(seed), 6)
    queries = scatter_about(streams_of[0], (TOKENS, HEADS * HD), 2.0, 8.0, ((0, 256),))
    key_vectors = scatter_about(streams_of[1], (TOKENS, HEADS * HD), 2.0, 8.0, ((0, 256),))
    value_vectors = scatter_about(streams_of[2], (TOKENS, HEADS * HD), 1.0, 6.0, ((0, 256),))
    out_grad = scatter_about(streams_of[3], (TOKENS, HEADS * HD), 1.0, 6.0, ((0, 256),))
    doc_ids = draw_doc_ids(jax.random.fold_in(streams_of[5], 71), 0)
    return {"queries": queries, "key_vectors": key_vectors, "value_vectors": value_vectors, "out_grad": out_grad, "doc_ids": doc_ids}


def feature_map(values):
    wide = values.astype(jnp.float32)
    return jnp.where(wide > 0, wide + 1.0, jnp.exp(jnp.minimum(wide, 0.0)))

def feature_slope(values):
    wide = values.astype(jnp.float32)
    return jnp.where(wide > 0, jnp.ones_like(wide), jnp.exp(jnp.minimum(wide, 0.0)))

def contract(form, left, right):
    return jnp.einsum(form, left, right, precision=lax.Precision.HIGHEST)

def settle(half):
    return lax.optimization_barrier(half).astype(jnp.float32)

def segment_sums(blocks, stretch_ids, backward):

    def advance(carry, item):
        running, previous = carry
        current, stretch_id = item
        running = jnp.where(stretch_id == previous, running, jnp.zeros_like(running))
        return ((running + current, stretch_id), running)
    start = (jnp.zeros(blocks.shape[1:], jnp.float32), jnp.array(-1, jnp.int32))
    final_carry, result = lax.scan(advance, start, (blocks, stretch_ids), reverse=backward)
    return result

def one_head(operands, stretch_ids):
    queries, key_vectors, value_vectors, out_grad = operands
    query_wide = settle(feature_map(queries).astype(jnp.bfloat16))
    key_wide = settle(feature_map(key_vectors).astype(jnp.bfloat16))
    value_wide = value_vectors.astype(jnp.float32)
    grad_wide = out_grad.astype(jnp.float32)
    causal = jnp.arange(STRETCH)[:, None] >= jnp.arange(STRETCH)[None, :]
    scores = settle(jnp.where(causal, contract('nta,nsa->nts', query_wide, key_wide), 0.0).astype(jnp.bfloat16))
    pair_states = contract('nsa,nsb->nab', key_wide, value_wide)
    prefix = segment_sums(pair_states, stretch_ids, False)
    raw = contract('nts,nsb->ntb', scores, value_wide) + contract('nta,nab->ntb', query_wide, prefix)
    rms_scale = jnp.sqrt(lax.optimization_barrier(jnp.mean(raw * raw, axis=-1, keepdims=True)) + 1e-06)
    normed = raw / rms_scale
    along = lax.optimization_barrier(jnp.mean(grad_wide * normed, axis=-1, keepdims=True))
    scaled = settle(((grad_wide - normed * along) / rms_scale).astype(jnp.bfloat16))
    mixed = settle(jnp.where(causal, contract('ntb,nsb->nts', scaled, value_wide), 0.0).astype(jnp.bfloat16))
    query_states = contract('nta,ntb->nab', query_wide, scaled)
    suffix = segment_sums(query_states, stretch_ids, True)
    query_grad = (contract('nts,nsa->nta', mixed, key_wide) + contract('ntb,nab->nta', scaled, prefix)) * feature_slope(queries)
    key_grad = (contract('nts,nta->nsa', mixed, query_wide) + contract('nsb,nab->nsa', value_wide, suffix)) * feature_slope(key_vectors)
    value_grad = contract('nts,ntb->nsb', scores, scaled) + contract('nsa,nab->nsb', key_wide, suffix)
    return (normed.astype(jnp.bfloat16), query_grad.astype(jnp.bfloat16), key_grad.astype(jnp.bfloat16), value_grad.astype(jnp.bfloat16))

def split_heads(array):
    return array.reshape(NCHUNK, STRETCH, HEADS, HD).transpose(2, 0, 1, 3)

def join_heads(array):
    return array.transpose(1, 2, 0, 3).reshape(TOKENS, HEADS * HD)

def reference(queries, key_vectors, value_vectors, out_grad, doc_ids):
    operands = (split_heads(queries), split_heads(key_vectors), split_heads(value_vectors), split_heads(out_grad))
    results = lax.map(partial(one_head, stretch_ids=doc_ids.astype(jnp.int32)), operands)
    return (join_heads(results[0]), join_heads(results[1]), join_heads(results[2]), join_heads(results[3]))
```

```python
import functools

import jax
import jax.numpy as jnp
from jax import lax
from jax.experimental import pallas as pl
from jax.experimental.pallas import tpu as pltpu
from jax.sharding import PartitionSpec as P

HD = 128
TAG = 16
MESH = pl.DeviceIdType.MESH
F32 = jnp.float32
BF16 = jnp.bfloat16


def feature(x):
    return jnp.where(x > 0, x + 1.0, jnp.exp(jnp.minimum(x, 0.0)))


def slope(x):
    return jnp.where(x > 0, jnp.ones_like(x), jnp.exp(jnp.minimum(x, 0.0)))


def dot_nn(a, b):
    return lax.dot_general(a, b, (((1,), (0,)), ((), ())), preferred_element_type=F32)


def dot_nt(a, b):
    return lax.dot_general(a, b, (((1,), (1,)), ((), ())), preferred_element_type=F32)


def dot_tn(a, b):
    return lax.dot_general(a, b, (((0,), (0,)), ((), ())), preferred_element_type=F32)


def kernel(
    ny,
    nx,
    nz,
    chunks,
    ids,
    q_ref,
    k_ref,
    v_ref,
    g_ref,
    att_ref,
    qg_ref,
    kg_ref,
    vg_ref,
    kf_buf,
    qf_buf,
    a_buf,
    sc_buf,
    kl_buf,
    vl_buf,
    s_out,
    s_in,
    p_out,
    p_in,
    g_out,
    g_in,
    t_out,
    t_in,
    u_out,
    u_in,
    send_a,
    recv_a,
    send_g,
    recv_g,
    send_t,
    recv_t,
    send_u,
    recv_u,
):
    ctx = lax.axis_index("ctx")
    z = lax.axis_index("head")
    core = lax.rem(ctx, 2)
    x = lax.rem(ctx // 2, nx)
    y = ctx // (2 * nx)

    def at(yy, xx, cc):
        return (yy * nx + xx) * 2 + cc

    peer = (at(y, x, 1 - core), z)
    lines = [(ctx, lax.rem(z + d, nz)) for d in range(1, nz)]
    rows = [(at(y, lax.rem(x + d, nx), core), z) for d in range(1, nx)]
    columns = [(at(lax.rem(y + d, ny), x, core), z) for d in range(1, ny)]
    everyone = lines + rows + columns + [peer]

    barrier = pltpu.get_barrier_semaphore()
    for device in everyone:
        pl.semaphore_signal(barrier, inc=1, device_id=device, device_id_type=MESH)

    core_one = (core == 1).astype(F32)
    doc = [ids[i] for i in range(nz)]
    causal = lax.broadcasted_iota(jnp.int32, (HD, HD), 0) >= lax.broadcasted_iota(
        jnp.int32, (HD, HD), 1
    )

    def alike(a, b):
        return jnp.where(a == b, 1.0, 0.0).astype(F32)

    def columns_of(h):
        return pl.ds(pl.multiple_of(h * HD, HD), HD)

    def remote(src, dst, send, recv, device):
        return pltpu.make_async_remote_copy(
            src_ref=src,
            dst_ref=dst,
            send_sem=send,
            recv_sem=recv,
            device_id=device,
            device_id_type=MESH,
        )

    def exchange(out, into, phase, j):
        into[j, z] = out[j, z]
        for device in lines:
            remote(
                out.at[j, device[1]],
                into.at[j, z],
                send_a.at[phase, j],
                recv_a.at[phase, j],
                device,
            ).start()

    def wait_in(into, sem, count):
        part = into.at[pl.ds(0, count)]
        pltpu.make_async_copy(part, part, sem).wait()

    def heads(body):
        def pair(i, carry):
            for u in range(2):
                body(i * 2 + u)
            return carry

        lax.fori_loop(0, nz // 2, pair, 0)

    def states(j):
        def one(o):
            h = nz * j + o
            c = columns_of(h)
            kf = feature(k_ref[:, c].astype(F32)).astype(BF16)
            kf_buf[h] = kf
            s_out[0, j, o] = dot_tn(kf, v_ref[:, c]).astype(BF16)

        heads(one)

    def before(j):
        def one(o):
            h = nz * j + o
            c = columns_of(h)
            qf = feature(q_ref[:, c].astype(F32)).astype(BF16)
            qf_buf[h] = qf
            a_buf[h] = jnp.where(causal, dot_nt(qf, kf_buf[h]), 0.0).astype(BF16)

        heads(one)

    def tag_of(message):
        return message[pl.ds(HD, TAG), :].astype(F32)[0:1, :]

    def value_of(message):
        return message[pl.ds(0, HD), :].astype(F32)

    def put(message, value, tag):
        message[pl.ds(0, HD), :] = value.astype(BF16)
        message[pl.ds(HD, TAG), :] = jnp.broadcast_to(tag, (TAG, HD)).astype(BF16)

    def group_sum(way, j):
        wait_in(s_in.at[way, j], recv_a.at[2 * way, j], nz - 1)
        edge = doc[nz - 1] if way == 0 else doc[0]
        total = jnp.zeros((HD, HD), F32)
        for i in range(nz):
            total = total + alike(doc[i], edge) * s_in[way, j, i].astype(F32)
        put(g_out.at[way, j], total, edge.astype(F32) * jnp.ones((1, HD), F32))
        remote(
            g_out.at[way, j], g_in.at[way, j], send_g.at[way, j], recv_g.at[way, j], peer
        ).start()

    def chip_sum(way, j):
        pltpu.make_async_copy(g_in.at[way, j], g_in.at[way, j], recv_g.at[way, j]).wait()
        mine, other = g_out.at[way, j], g_in.at[way, j]
        late = core_one if way == 0 else 1.0 - core_one
        same = alike(tag_of(mine), tag_of(other))
        keep_mine = late + (1.0 - late) * same
        keep_other = (1.0 - late) + late * same
        put(
            t_out.at[way, j],
            keep_mine * value_of(mine) + keep_other * value_of(other),
            late * tag_of(mine) + (1.0 - late) * tag_of(other),
        )
        for d, device in enumerate(rows):
            remote(
                t_out.at[way, j],
                t_in.at[way, j, d],
                send_t.at[way, j],
                recv_t.at[way, j],
                device,
            ).start()

    def row_sum(way, j):
        wait_in(t_in.at[way, j], recv_t.at[way, j], nx - 1)
        edge = nx - 1 if way == 0 else 0
        parts = [(t_out.at[way, j], x)] + [
            (t_in.at[way, j, d], lax.rem(x + nx - 1 - d, nx)) for d in range(nx - 1)
        ]
        tag = jnp.zeros((1, HD), F32)
        for part, place in parts:
            tag = tag + alike(place, edge) * tag_of(part)
        total = jnp.zeros((HD, HD), F32)
        for part, place in parts:
            total = total + alike(tag_of(part), tag) * value_of(part)
        put(u_out.at[way, j], total, tag)
        for d, device in enumerate(columns):
            remote(
                u_out.at[way, j],
                u_in.at[way, j, d],
                send_u.at[way, j],
                recv_u.at[way, j],
                device,
            ).start()

    def hand_back(way, j):
        wait_in(u_in.at[way, j], recv_u.at[way, j], ny - 1)
        want = (doc[0] if way == 0 else doc[nz - 1]).astype(F32)
        late = core_one if way == 0 else 1.0 - core_one
        other = g_in.at[way, j]
        running = late * alike(tag_of(other), want) * value_of(other)
        for d in range(nx - 1):
            before_me = (x >= d + 1) if way == 0 else (x < d + 1)
            part = t_in.at[way, j, d]
            running = running + before_me.astype(F32) * alike(tag_of(part), want) * value_of(part)
        for d in range(ny - 1):
            before_me = (y >= d + 1) if way == 0 else (y < d + 1)
            part = u_in.at[way, j, d]
            running = running + before_me.astype(F32) * alike(tag_of(part), want) * value_of(part)
        order = list(range(nz)) if way == 0 else list(range(nz - 1, -1, -1))
        for n, i in enumerate(order):
            p_out[way, j, i] = running.astype(BF16)
            if n < nz - 1:
                running = alike(doc[i], doc[order[n + 1]]) * (
                    running + s_in[way, j, i].astype(F32)
                )
        exchange(p_out.at[way], p_in.at[way], 2 * way + 1, j)

    def middle(j):
        wait_in(p_in.at[0, j], recv_a.at[1, j], nz - 1)

        def one(o):
            h = nz * j + o
            c = columns_of(h)
            qf = qf_buf[h]
            raw = dot_nn(a_buf[h], v_ref[:, c]) + dot_nn(qf, p_in[0, j, o])
            inverse = lax.rsqrt(jnp.mean(raw * raw, axis=-1, keepdims=True) + 1e-06)
            normed = raw * inverse
            att_ref[:, c] = normed.astype(BF16)
            wide = g_ref[:, c].astype(F32)
            along = jnp.mean(wide * normed, axis=-1, keepdims=True)
            scaled = ((wide - normed * along) * inverse).astype(BF16)
            sc_buf[h] = scaled
            s_out[1, j, o] = dot_tn(qf, scaled).astype(BF16)

        heads(one)
        exchange(s_out.at[1], s_in.at[1], 2, j)

    def after(j):
        def one(o):
            h = nz * j + o
            c = columns_of(h)
            scaled = sc_buf[h]
            mixed = jnp.where(causal, dot_nt(scaled, v_ref[:, c]), 0.0).astype(BF16)
            grad = dot_nn(mixed, kf_buf[h]) + dot_nt(scaled, p_in[0, j, o])
            qg_ref[:, c] = (grad * slope(q_ref[:, c].astype(F32))).astype(BF16)
            kl_buf[h] = dot_tn(mixed, qf_buf[h])
            vl_buf[h] = dot_tn(a_buf[h], scaled)

        heads(one)

    def finish(j):
        wait_in(p_in.at[1, j], recv_a.at[3, j], nz - 1)

        def one(o):
            h = nz * j + o
            c = columns_of(h)
            state = p_in[1, j, o]
            grad = kl_buf[h] + dot_nt(v_ref[:, c], state)
            kg_ref[:, c] = (grad * slope(k_ref[:, c].astype(F32))).astype(BF16)
            vg_ref[:, c] = (vl_buf[h] + dot_nn(kf_buf[h], state)).astype(BF16)

        heads(one)

    last = chunks - 1
    states(0)
    pl.semaphore_wait(barrier, len(everyone))
    exchange(s_out.at[0], s_in.at[0], 0, 0)
    for j in range(1, chunks):
        states(j)
        exchange(s_out.at[0], s_in.at[0], 0, j)
    for j in range(chunks):
        before(j)
    for step in range(chunks + 3):
        if step < chunks:
            group_sum(0, step)
        if 0 <= step - 1 < chunks:
            chip_sum(0, step - 1)
        if 0 <= step - 2 < chunks:
            row_sum(0, step - 2)
        if 0 <= step - 3 < chunks:
            hand_back(0, step - 3)
    for j in range(chunks):
        middle(j)
        if j < last:
            after(j)
    for step in range(chunks + 3):
        if step < chunks:
            group_sum(1, step)
        if step == 0:
            after(last)
        if 0 <= step - 1 < chunks:
            chip_sum(1, step - 1)
        if 0 <= step - 2 < chunks:
            row_sum(1, step - 2)
        if 0 <= step - 3 < chunks:
            hand_back(1, step - 3)
    for j in range(chunks):
        finish(j)

    for way in range(2):
        for j in range(chunks):
            wait_in(s_in.at[way, j], send_a.at[2 * way, j], nz - 1)
            wait_in(p_in.at[way, j], send_a.at[2 * way + 1, j], nz - 1)
            pltpu.make_async_copy(g_in.at[way, j], g_in.at[way, j], send_g.at[way, j]).wait()
            wait_in(t_in.at[way, j], send_t.at[way, j], nx - 1)
            wait_in(u_in.at[way, j], send_u.at[way, j], ny - 1)


def shards(ny, nx, queries, key_vectors, value_vectors, out_grad, doc_ids):
    nz = lax.axis_size("head")
    tokens, features = queries.shape
    count = features // HD
    chunks = count // nz
    vmem = pl.BlockSpec(memory_space=pltpu.VMEM)
    half = functools.partial(pltpu.VMEM, dtype=BF16)
    wide = functools.partial(pltpu.VMEM, dtype=F32)
    dma = pltpu.SemaphoreType.DMA
    message = (HD + TAG, HD)
    out = jax.ShapeDtypeStruct((tokens, features), BF16)
    return pl.pallas_call(
        functools.partial(kernel, ny, nx, nz, chunks),
        out_shape=(out,) * 4,
        in_specs=[pl.BlockSpec(memory_space=pltpu.SMEM)] + [vmem] * 4,
        out_specs=(vmem,) * 4,
        scratch_shapes=[
            half((count, HD, HD)),
            half((count, HD, HD)),
            half((count, HD, HD)),
            half((count, HD, HD)),
            wide((count, HD, HD)),
            wide((count, HD, HD)),
            half((2, chunks, nz, HD, HD)),
            half((2, chunks, nz, HD, HD)),
            half((2, chunks, nz, HD, HD)),
            half((2, chunks, nz, HD, HD)),
            half((2, chunks, *message)),
            half((2, chunks, *message)),
            half((2, chunks, *message)),
            half((2, chunks, nx - 1, *message)),
            half((2, chunks, *message)),
            half((2, chunks, ny - 1, *message)),
            dma((4, chunks)),
            dma((4, chunks)),
            dma((2, chunks)),
            dma((2, chunks)),
            dma((2, chunks)),
            dma((2, chunks)),
            dma((2, chunks)),
            dma((2, chunks)),
        ],
        compiler_params=pltpu.CompilerParams(
            collective_id=0, has_side_effects=True, vmem_limit_bytes=48 * 2**20
        ),
    )(doc_ids, queries, key_vectors, value_vectors, out_grad)


def build(mesh, ny, nx):
    spec = P(("ctx", "head"), None)
    return jax.shard_map(
        functools.partial(shards, ny, nx),
        mesh=mesh,
        in_specs=(spec,) * 4 + (P("ctx"),),
        out_specs=(spec,) * 4,
        check_vma=False,
    )


def solution(mesh):
    return build(mesh, 4, 4)
```

```python
import functools

import jax
import jax.numpy as jnp
from jax import lax
from jax.experimental import pallas as pl
from jax.experimental.pallas import tpu as pltpu
from jax.sharding import PartitionSpec as P

HD = 128
TAG = 16
MESH = pl.DeviceIdType.MESH
F32 = jnp.float32
BF16 = jnp.bfloat16


def feature(x):
    return jnp.where(x > 0, x + 1.0, jnp.exp(jnp.minimum(x, 0.0)))


def slope(x):
    return jnp.where(x > 0, jnp.ones_like(x), jnp.exp(jnp.minimum(x, 0.0)))


def dot_nn(a, b):
    return lax.dot_general(a, b, (((1,), (0,)), ((), ())), preferred_element_type=F32)


def dot_nt(a, b):
    return lax.dot_general(a, b, (((1,), (1,)), ((), ())), preferred_element_type=F32)


def dot_tn(a, b):
    return lax.dot_general(a, b, (((0,), (0,)), ((), ())), preferred_element_type=F32)


def plan(chunks):
    if chunks == 4:
        order = [
            "S0 T0 B0 S1",
            "T1 B1 S2 C0",
            "T2 C1 B2 S3",
            "G0 T3 C2 X0",
            "G1 X1 Y0 C3",
            "G2 X2 Y1 H0",
            "B3 G3 Y2 X3",
            "H1 E0 Y3 H2",
            "E1 H3 N0 M0",
            "N1 E2 N2 E3",
            "c0 M2 A2 M1",
            "M3 g0 x0 c2",
            "c1 y0 N3 c3",
            "g2 x2 h0 g1",
            "x1 g3 y2 x3",
            "e0 y1 A3 h2",
            "y3 h1 h3 A0",
            "F0 e2 O2 e1",
            "e3 A1 F2 O0",
            "O3 F1 O1 F3",
        ]
        return " ".join(order).split()
    return [f"{step}{j}" for step in "STBCGXYHENMAcgxyheOF" for j in range(chunks)]


def kernel(
    ny,
    nx,
    nz,
    chunks,
    ids,
    q_hbm,
    k_hbm,
    v_hbm,
    g_hbm,
    att_ref,
    qg_ref,
    kg_ref,
    vg_ref,
    q_ref,
    k_ref,
    v_ref,
    g_ref,
    load_sem,
    kf_buf,
    qf_buf,
    a_buf,
    sc_buf,
    kl_buf,
    vl_buf,
    s_out,
    leaf_in,
    up_out,
    up_in,
    p_out,
    p_in,
    aux_in,
    ex_out,
    g_out,
    g_in,
    t_out,
    t_in,
    u_out,
    u_in,
    send_a,
    recv_a,
    send_more,
    recv_more,
    send_g,
    recv_g,
    send_t,
    recv_t,
    send_u,
    recv_u,
):
    ctx = lax.axis_index("ctx")
    z = lax.axis_index("head")
    core = lax.rem(ctx, 2)
    x = lax.rem(ctx // 2, nx)
    y = ctx // (2 * nx)

    def at(yy, xx, cc):
        return (yy * nx + xx) * 2 + cc

    peer = (at(y, x, 1 - core), z)
    lines = [(ctx, lax.rem(z + d, nz)) for d in (1, 2, nz - 1, nz - 2)]
    rows = [(at(y, lax.rem(x + d, nx), core), z) for d in range(1, nx)]
    columns = [(at(lax.rem(y + d, ny), x, core), z) for d in range(1, ny)]
    everyone = lines + rows + columns + [peer]

    barrier = pltpu.get_barrier_semaphore()
    for device in everyone:
        pl.semaphore_signal(barrier, inc=1, device_id=device, device_id_type=MESH)

    def block(ref, j):
        return ref.at[:, pl.ds(j * nz * HD, nz * HD)]

    def load(i, j):
        hbm, ref = ((k_hbm, k_ref), (v_hbm, v_ref), (q_hbm, q_ref), (g_hbm, g_ref))[i]
        return pltpu.make_async_copy(block(hbm, j), block(ref, j), load_sem.at[i, j])

    for i in range(0, 4, 2):
        for j in range(chunks):
            load(i, j).start()
            load(i + 1, j).start()

    core_one = (core == 1).astype(F32)
    doc = [ids[i] for i in range(nz)]
    causal = lax.broadcasted_iota(jnp.int32, (HD, HD), 0) >= lax.broadcasted_iota(
        jnp.int32, (HD, HD), 1
    )

    def alike(a, b):
        return jnp.where(a == b, 1.0, 0.0).astype(F32)

    def place(way):
        return z if way == 0 else nz - 1 - z

    def line(way, v):
        v = lax.rem(v + 2 * nz, nz)
        return (ctx, v if way == 0 else nz - 1 - v)

    def doc_at(way, v):
        v = lax.rem(v + 2 * nz, nz)
        return ids[v if way == 0 else nz - 1 - v]

    def following(way, v):
        return doc_at(way, jnp.minimum(v + 1, nz - 1))

    def slot(v):
        return lax.rem(v + 2 * nz, nz)

    def head_slot(way, o):
        return o if way == 0 else nz - 1 - o

    def columns_of(h):
        return pl.ds(pl.multiple_of(h * HD, HD), HD)

    def remote(src, dst, send, recv, device):
        return pltpu.make_async_remote_copy(
            src_ref=src,
            dst_ref=dst,
            send_sem=send,
            recv_sem=recv,
            device_id=device,
            device_id_type=MESH,
        )

    def wait_in(into, sem, count):
        part = into.at[pl.ds(0, count)]
        pltpu.make_async_copy(part, part, sem).wait()

    def near(body):
        for off in (0, 1, 2, nz - 2, nz - 1):
            body(lax.rem(z + off, nz))

    def far(body):
        for off in range(3, nz - 2):
            body(lax.rem(z + off, nz))

    def every(body):
        for o in range(nz):
            body(o)

    def states(j, some):
        def one(o):
            h = nz * j + o
            c = columns_of(h)
            kf = feature(k_ref[:, c].astype(F32)).astype(BF16)
            kf_buf[h] = kf
            s_out[0, j, o] = dot_tn(kf, v_ref[:, c]).astype(BF16)

        some(one)

    def before(j):
        load(2, j).wait()
        load(3, j).wait()

        def one(o):
            h = nz * j + o
            c = columns_of(h)
            qf = feature(q_ref[:, c].astype(F32)).astype(BF16)
            qf_buf[h] = qf
            a_buf[h] = jnp.where(causal, dot_nt(qf, kf_buf[h]), 0.0).astype(BF16)

        every(one)

    averaging = jnp.full((HD, HD), 1.0 / HD, BF16)

    def row_mean(product):
        return dot_nn(product.astype(BF16), averaging)

    def tag_of(message):
        return message[pl.ds(HD, TAG), :].astype(F32)[0:1, :]

    def value_of(message):
        return message[pl.ds(0, HD), :].astype(F32)

    def put(message, value, tag):
        message[pl.ds(0, HD), :] = value.astype(BF16)
        message[pl.ds(HD, TAG), :] = jnp.broadcast_to(tag, (TAG, HD)).astype(BF16)

    def send_to(src, dst, way, phase, j, device):
        remote(src, dst, send_a.at[way, phase, j], recv_a.at[way, phase, j], device).start()

    def send_more_to(src, dst, way, phase, j, device):
        remote(
            src, dst, send_more.at[way, phase, j], recv_more.at[way, phase, j], device
        ).start()

    def one_more(way, phase, j, sem):
        part = aux_in.at[way, j, 0]
        pltpu.make_async_copy(part, part, sem.at[way, phase, j]).wait()

    def spread(way, j):
        v = place(way)
        source = s_out.at[way, j]
        into = leaf_in.at[way, j]
        send_to(source.at[slot(v - 4)], into.at[1], way, 0, j, line(way, v - 2))
        send_to(source.at[slot(v - 3)], into.at[0], way, 0, j, line(way, v - 1))
        send_to(source.at[slot(v + 3)], into.at[2], way, 0, j, line(way, v + 1))

    def collect(way, j):
        v = place(way)
        alone = alike(doc_at(way, v), following(way, v))
        mine, up, into = s_out.at[way, j], up_out.at[way, j], up_in.at[way, j]

        def state(u):
            return mine[slot(u)].astype(F32)

        up[0] = (alone * state(v - 1)).astype(BF16)
        up[1] = (alone * state(v + 1)).astype(BF16)
        into[v] = (alone * state(v)).astype(BF16)
        send_to(up.at[0], into.at[v], way, 1, j, line(way, v - 1))
        send_to(up.at[1], into.at[v], way, 1, j, line(way, v + 1))
        wait_in(leaf_in.at[way, j], recv_a.at[way, 0, j], 3)
        first, second, behind = (leaf_in[way, j, i].astype(F32) for i in range(3))
        after_run = following(way, jnp.minimum(v + 2, nz - 1))

        def weight(inside, u, target):
            return inside.astype(F32) * alike(doc_at(way, u), target)

        up[2] = (
            alike(doc_at(way, v), after_run) * state(v - 2)
            + weight(v + 1 < nz, v + 1, after_run) * first
            + weight(v + 2 < nz, v + 2, after_run) * second
        ).astype(BF16)
        send_to(up.at[2], into.at[v], way, 1, j, line(way, v - 2))
        up[3] = (
            alone * state(v + 2) + weight(v > 0, v - 1, following(way, v)) * behind
        ).astype(BF16)
        send_to(up.at[3], into.at[jnp.maximum(v - 1, 0)], way, 1, j, line(way, v + 2))

        @pl.when(v >= nz - 2)
        def _():
            target = doc_at(way, v + 3)
            up[4] = (
                weight(v + 1 >= nz, v + 1, target) * first
                + weight(v + 2 >= nz, v + 2, target) * second
            ).astype(BF16)
            send_more_to(up.at[4], into.at[0], way, 0, j, line(way, v - 2))

        @pl.when(v == 0)
        def _():
            up[4] = leaf_in[way, j, 2]
            send_more_to(up.at[4], into.at[nz - 1], way, 0, j, line(way, v + 2))

    def segments(way):
        v = place(way)
        result = []
        for i in range(nz):
            off = lax.rem(i - v + nz, nz)
            length = jnp.where(off == 2, 3, jnp.where(off == 5, 2, 1))
            inner = (off == 3) | (off == 4) | (off == 6)
            if i == 0:
                length = jnp.where(off == 3, 2, length)
                start = None
                keep = alike(doc_at(way, i), following(way, i + length - 1))
            else:
                start = jnp.logical_not(inner)
                end = jnp.minimum(i + length - 1, nz - 1)
                keep = jnp.where(inner, 1.0, alike(doc_at(way, i), following(way, end)))
            result.append((start, keep))
        return result

    def part_of(way, j, i, start):
        value = up_in[way, j, i].astype(F32)
        return value if start is None else jnp.where(start, value, 0.0)

    def group_sum(way, j):
        v = place(way)
        wait_in(up_in.at[way, j], recv_a.at[way, 1, j], 4)

        @pl.when((v == 2) | (v == 4) | (v == 5))
        def _():
            one_more(way, 0, j, recv_more)

        total = jnp.zeros((HD, HD), F32)
        for i, (start, keep) in enumerate(segments(way)):
            total = keep * total + part_of(way, j, i, start)
        edge = doc_at(way, nz - 1)
        put(g_out.at[way, j], total, edge.astype(F32) * jnp.ones((1, HD), F32))
        remote(
            g_out.at[way, j], g_in.at[way, j], send_g.at[way, j], recv_g.at[way, j], peer
        ).start()

    def chip_sum(way, j):
        pltpu.make_async_copy(g_in.at[way, j], g_in.at[way, j], recv_g.at[way, j]).wait()
        mine, other = g_out.at[way, j], g_in.at[way, j]
        late = core_one if way == 0 else 1.0 - core_one
        same = alike(tag_of(mine), tag_of(other))
        keep_mine = late + (1.0 - late) * same
        keep_other = (1.0 - late) + late * same
        put(
            t_out.at[way, j],
            keep_mine * value_of(mine) + keep_other * value_of(other),
            late * tag_of(mine) + (1.0 - late) * tag_of(other),
        )
        for d, device in enumerate(rows):
            remote(
                t_out.at[way, j],
                t_in.at[way, j, d],
                send_t.at[way, j],
                recv_t.at[way, j],
                device,
            ).start()

    def row_sum(way, j):
        if nx > 1:
            wait_in(t_in.at[way, j], recv_t.at[way, j], nx - 1)
        edge = nx - 1 if way == 0 else 0
        parts = [(t_out.at[way, j], x)] + [
            (t_in.at[way, j, d], lax.rem(x + nx - 1 - d, nx)) for d in range(nx - 1)
        ]
        tag = jnp.zeros((1, HD), F32)
        for part, place in parts:
            tag = tag + alike(place, edge) * tag_of(part)
        total = jnp.zeros((HD, HD), F32)
        for part, place in parts:
            total = total + alike(tag_of(part), tag) * value_of(part)
        put(u_out.at[way, j], total, tag)
        for d, device in enumerate(columns):
            remote(
                u_out.at[way, j],
                u_in.at[way, j, d],
                send_u.at[way, j],
                recv_u.at[way, j],
                device,
            ).start()

    def hand_back(way, j):
        if ny > 1:
            wait_in(u_in.at[way, j], recv_u.at[way, j], ny - 1)
        want = (doc[0] if way == 0 else doc[nz - 1]).astype(F32)
        late = core_one if way == 0 else 1.0 - core_one
        other = g_in.at[way, j]
        running = late * alike(tag_of(other), want) * value_of(other)
        for d in range(nx - 1):
            before_me = (x >= d + 1) if way == 0 else (x < d + 1)
            part = t_in.at[way, j, d]
            running = running + before_me.astype(F32) * alike(tag_of(part), want) * value_of(part)
        for d in range(ny - 1):
            before_me = (y >= d + 1) if way == 0 else (y < d + 1)
            part = u_in.at[way, j, d]
            running = running + before_me.astype(F32) * alike(tag_of(part), want) * value_of(part)
        v = place(way)
        for i, (start, keep) in enumerate(segments(way)):
            p_out[way, j, i] = running.astype(BF16)
            if i < nz - 1:
                running = keep * running + part_of(way, j, i, start)
        out, into, aux = p_out.at[way, j], p_in.at[way, j], aux_in.at[way, j]
        behind = jnp.where(slot(v - 2) == 0, 0, slot(v - 3))
        send_to(out.at[behind], aux.at[0], way, 2, j, line(way, v - 2))
        send_to(out.at[slot(v + 2)], into.at[v], way, 2, j, line(way, v + 2))

        @pl.when((v == 4) | (v == 5))
        def _():
            send_more_to(out.at[0], aux.at[1], way, 1, j, line(way, v + 2))

        @pl.when(v == 2)
        def _():
            send_more_to(out.at[nz - 1], aux.at[1], way, 1, j, line(way, v - 2))

        send_to(out.at[slot(v - 1)], into.at[v], way, 2, j, line(way, v - 1))
        send_to(out.at[slot(v + 1)], into.at[v], way, 2, j, line(way, v + 1))
        p_in[way, j, v] = p_out[way, j, v]

    def expand(way, j):
        v = place(way)
        wait_in(p_in.at[way, j], recv_a.at[way, 2, j], 4)
        more = (v >= nz - 2) | (v == 0)

        @pl.when(more)
        def _():
            one_more(way, 1, j, recv_more)

        mine, leaf, aux, out = s_out.at[way, j], leaf_in.at[way, j], aux_in.at[way, j], ex_out.at[way, j]

        def step(u, value, state):
            return alike(doc_at(way, u), doc_at(way, u + 1)) * (value + state.astype(F32))

        extra = jnp.where(more, aux[1].astype(F32), 0.0)
        here = p_in[way, j, slot(v - 2)].astype(F32)
        one = jnp.where(v + 1 == nz, extra, step(v, here, mine[slot(v - 2)]))
        two = jnp.where(v + 2 == nz, extra, step(v + 1, one, leaf[0]))
        out[1] = two.astype(BF16)
        send_to(out.at[1], p_in.at[way, j, slot(v - 2)], way, 3, j, line(way, v + 2))
        out[0] = one.astype(BF16)
        send_to(out.at[0], p_in.at[way, j, slot(v - 2)], way, 3, j, line(way, v + 1))
        begin = aux[0].astype(F32)
        out[2] = jnp.where(v == 0, extra, begin).astype(BF16)
        send_to(out.at[2], p_in.at[way, j, slot(v + 2)], way, 3, j, line(way, v - 1))
        own = jnp.where(v == 0, begin, step(v - 1, begin, leaf[2]))
        p_in[way, j, slot(v + 2)] = own.astype(BF16)

    def middle(j, some):
        def one(o):
            h = nz * j + o
            c = columns_of(h)
            qf = qf_buf[h]
            raw = dot_nn(a_buf[h], v_ref[:, c]) + dot_nn(qf, p_in[0, j, o])
            inverse = lax.rsqrt(row_mean(raw * raw) + 1e-06)
            normed = raw * inverse
            att_ref[:, c] = normed.astype(BF16)
            wide = g_ref[:, c].astype(F32)
            along = row_mean(wide * normed)
            scaled = ((wide - normed * along) * inverse).astype(BF16)
            sc_buf[h] = scaled
            s_out[1, j, nz - 1 - o] = dot_tn(qf, scaled).astype(BF16)

        some(one)

    def middle_far(j):
        wait_in(p_in.at[0, j], recv_a.at[0, 3, j], 3)
        middle(j, far)
        spread(1, j)

    def after(j):
        def one(o):
            h = nz * j + o
            c = columns_of(h)
            scaled = sc_buf[h]
            mixed = jnp.where(causal, dot_nt(scaled, v_ref[:, c]), 0.0).astype(BF16)
            grad = dot_nn(mixed, kf_buf[h]) + dot_nt(scaled, p_in[0, j, o])
            qg_ref[:, c] = (grad * slope(q_ref[:, c].astype(F32))).astype(BF16)
            kl_buf[h] = dot_tn(mixed, qf_buf[h])
            vl_buf[h] = dot_tn(a_buf[h], scaled)

        every(one)

    def finish(j, some):
        def one(o):
            h = nz * j + o
            c = columns_of(h)
            state = p_in[1, j, nz - 1 - o]
            grad = kl_buf[h] + dot_nt(v_ref[:, c], state)
            kg_ref[:, c] = (grad * slope(k_ref[:, c].astype(F32))).astype(BF16)
            vg_ref[:, c] = (vl_buf[h] + dot_nn(kf_buf[h], state)).astype(BF16)

        some(one)

    def finish_far(j):
        wait_in(p_in.at[1, j], recv_a.at[1, 3, j], 3)
        finish(j, far)

    def start_states(j):
        load(0, j).wait()
        load(1, j).wait()
        states(j, far)
        if j == 0:
            pl.semaphore_wait(barrier, len(everyone))
        spread(0, j)

    steps = {
        "S": start_states,
        "B": before,
        "T": lambda j: states(j, near),
        "N": lambda j: middle(j, near),
        "M": middle_far,
        "A": after,
        "O": lambda j: finish(j, near),
        "F": finish_far,
        "C": functools.partial(collect, 0),
        "E": functools.partial(expand, 0),
        "c": functools.partial(collect, 1),
        "e": functools.partial(expand, 1),
        "G": functools.partial(group_sum, 0),
        "X": functools.partial(chip_sum, 0),
        "Y": functools.partial(row_sum, 0),
        "H": functools.partial(hand_back, 0),
        "g": functools.partial(group_sum, 1),
        "x": functools.partial(chip_sum, 1),
        "y": functools.partial(row_sum, 1),
        "h": functools.partial(hand_back, 1),
    }
    for step in plan(chunks):
        steps[step[0]](int(step[1:]))

    for way in range(2):
        v = place(way)
        for j in range(chunks):
            for phase, count in enumerate((3, 4, 4, 3)):
                wait_in(p_in.at[way, j], send_a.at[way, phase, j], count)
            pltpu.make_async_copy(g_in.at[way, j], g_in.at[way, j], send_g.at[way, j]).wait()
            if nx > 1:
                wait_in(t_in.at[way, j], send_t.at[way, j], nx - 1)
            if ny > 1:
                wait_in(u_in.at[way, j], send_u.at[way, j], ny - 1)

            @pl.when((v >= nz - 2) | (v == 0))
            def _():
                one_more(way, 0, j, send_more)

            @pl.when((v == 2) | (v == 4) | (v == 5))
            def _():
                one_more(way, 1, j, send_more)


def shards(ny, nx, queries, key_vectors, value_vectors, out_grad, doc_ids):
    nz = lax.axis_size("head")
    tokens, features = queries.shape
    count = features // HD
    chunks = count // nz
    anywhere = pl.BlockSpec(memory_space=pl.ANY)
    half = functools.partial(pltpu.VMEM, dtype=BF16)
    wide = functools.partial(pltpu.VMEM, dtype=F32)
    dma = pltpu.SemaphoreType.DMA
    message = (HD + TAG, HD)
    out = pltpu.VMEM((tokens, features), BF16)
    return pl.pallas_call(
        functools.partial(kernel, ny, nx, nz, chunks),
        out_shape=(out,) * 4,
        in_specs=[pl.BlockSpec(memory_space=pltpu.SMEM)] + [anywhere] * 4,
        out_specs=(pl.BlockSpec(memory_space=pltpu.VMEM),) * 4,
        scratch_shapes=[half((tokens, features))] * 4
        + [dma((4, chunks))]
        + [
            half((count, HD, HD)),
            half((count, HD, HD)),
            half((count, HD, HD)),
            half((count, HD, HD)),
            wide((count, HD, HD)),
            wide((count, HD, HD)),
            half((2, chunks, nz, HD, HD)),
            half((2, chunks, 3, HD, HD)),
            half((2, chunks, 5, HD, HD)),
            half((2, chunks, nz, HD, HD)),
            half((2, chunks, nz, HD, HD)),
            half((2, chunks, nz, HD, HD)),
            half((2, chunks, 2, HD, HD)),
            half((2, chunks, 3, HD, HD)),
            half((2, chunks, *message)),
            half((2, chunks, *message)),
            half((2, chunks, *message)),
            half((2, chunks, max(nx - 1, 1), *message)),
            half((2, chunks, *message)),
            half((2, chunks, max(ny - 1, 1), *message)),
            dma((2, 4, chunks)),
            dma((2, 4, chunks)),
            dma((2, 2, chunks)),
            dma((2, 2, chunks)),
            dma((2, chunks)),
            dma((2, chunks)),
            dma((2, chunks)),
            dma((2, chunks)),
            dma((2, chunks)),
            dma((2, chunks)),
        ],
        compiler_params=pltpu.CompilerParams(
            collective_id=0, has_side_effects=True, vmem_limit_bytes=56 * 2**20
        ),
    )(doc_ids, queries, key_vectors, value_vectors, out_grad)


def build(mesh, ny, nx):
    spec = P(("ctx", "head"), None)
    return jax.shard_map(
        functools.partial(shards, ny, nx),
        mesh=mesh,
        in_specs=(spec,) * 4 + (P("ctx"),),
        out_specs=(spec,) * 4,
        check_vma=False,
    )


def solution(mesh):
    return build(mesh, 4, 4)
```

```python
import functools

import jax
import jax.numpy as jnp
from jax import lax
from jax.experimental import pallas as pl
from jax.experimental.pallas import tpu as pltpu
from jax.sharding import PartitionSpec as P

HD = 128
TAG = 16
MESH = pl.DeviceIdType.MESH
F32 = jnp.float32
BF16 = jnp.bfloat16


def feature(x):
    return jnp.where(x > 0, x + 1.0, jnp.exp(jnp.minimum(x, 0.0)))


def slope(x):
    return jnp.where(x > 0, jnp.ones_like(x), jnp.exp(jnp.minimum(x, 0.0)))


def dot_nn(a, b):
    return lax.dot_general(a, b, (((1,), (0,)), ((), ())), preferred_element_type=F32)


def dot_nt(a, b):
    return lax.dot_general(a, b, (((1,), (1,)), ((), ())), preferred_element_type=F32)


def dot_tn(a, b):
    return lax.dot_general(a, b, (((0,), (0,)), ((), ())), preferred_element_type=F32)


def plan(chunks):
    if chunks == 4:
        order = [
            "S0 S3 T3 T0",
            "B0 S1 T1 S2",
            "C3 C1 T2 B3",
            "B2 C0 G3 B1",
            "C2 X3 G1 X1",
            "G0 Y3 X0 G2",
            "Y1 X2 H3 Y0",
            "H1 Y2 H0 H2",
            "E1 E0 N0 E3",
            "E2 M1 M0 N1",
            "M3 M2 N2 c1",
            "N3 c0 A0 A1",
            "c3 g1 x1 c2",
            "g0 A2 x0 g3",
            "y1 x3 g2 y0",
            "x2 y3 h1 h0",
            "y2 h3 h2 e0",
            "O0 e1 O1 e3",
            "A3 e2 O2 F1",
            "F0 O3 F3 F2",
        ]
        return " ".join(order).split()
    return [f"{step}{j}" for step in "STBCGXYHENMAcgxyheOF" for j in range(chunks)]


def kernel(
    ny,
    nx,
    nz,
    chunks,
    ids,
    q_hbm,
    k_hbm,
    v_hbm,
    g_hbm,
    att_ref,
    qg_ref,
    kg_ref,
    vg_ref,
    q_ref,
    k_ref,
    v_ref,
    g_ref,
    load_sem,
    kf_buf,
    qf_buf,
    a_buf,
    sc_buf,
    kl_buf,
    vl_buf,
    s_out,
    leaf_in,
    up_out,
    up_in,
    p_out,
    p_in,
    aux_in,
    ex_out,
    g_out,
    g_in,
    t_out,
    t_in,
    u_out,
    u_in,
    send_a,
    recv_a,
    send_more,
    recv_more,
    send_g,
    recv_g,
    send_t,
    recv_t,
    send_u,
    recv_u,
):
    ctx = lax.axis_index("ctx")
    z = lax.axis_index("head")
    core = lax.rem(ctx, 2)
    x = lax.rem(ctx // 2, nx)
    y = ctx // (2 * nx)

    def at(yy, xx, cc):
        return (yy * nx + xx) * 2 + cc

    peer = (at(y, x, 1 - core), z)
    lines = [(ctx, lax.rem(z + d, nz)) for d in (1, 2, nz - 1, nz - 2)]
    rows = [(at(y, lax.rem(x + d, nx), core), z) for d in range(1, nx)]
    columns = [(at(lax.rem(y + d, ny), x, core), z) for d in range(1, ny)]
    everyone = lines + rows + columns + [peer]

    barrier = pltpu.get_barrier_semaphore()
    for device in everyone:
        pl.semaphore_signal(barrier, inc=1, device_id=device, device_id_type=MESH)

    def block(ref, j):
        return ref.at[:, pl.ds(j * nz * HD, nz * HD)]

    def load(i, j):
        hbm, ref = ((k_hbm, k_ref), (v_hbm, v_ref), (q_hbm, q_ref), (g_hbm, g_ref))[i]
        return pltpu.make_async_copy(block(hbm, j), block(ref, j), load_sem.at[i, j])

    for i in range(0, 4, 2):
        for j in range(chunks):
            load(i, j).start()
            load(i + 1, j).start()

    core_one = (core == 1).astype(F32)
    doc = [ids[i] for i in range(nz)]
    causal = lax.broadcasted_iota(jnp.int32, (HD, HD), 0) >= lax.broadcasted_iota(
        jnp.int32, (HD, HD), 1
    )

    def alike(a, b):
        return jnp.where(a == b, 1.0, 0.0).astype(F32)

    def place(way):
        return z if way == 0 else nz - 1 - z

    def line(way, v):
        v = lax.rem(v + 2 * nz, nz)
        return (ctx, v if way == 0 else nz - 1 - v)

    def doc_at(way, v):
        v = lax.rem(v + 2 * nz, nz)
        return ids[v if way == 0 else nz - 1 - v]

    def following(way, v):
        return doc_at(way, jnp.minimum(v + 1, nz - 1))

    def slot(v):
        return lax.rem(v + 2 * nz, nz)

    def head_slot(way, o):
        return o if way == 0 else nz - 1 - o

    def columns_of(h):
        return pl.ds(pl.multiple_of(h * HD, HD), HD)

    def remote(src, dst, send, recv, device):
        return pltpu.make_async_remote_copy(
            src_ref=src,
            dst_ref=dst,
            send_sem=send,
            recv_sem=recv,
            device_id=device,
            device_id_type=MESH,
        )

    def wait_in(into, sem, count):
        part = into.at[pl.ds(0, count)]
        pltpu.make_async_copy(part, part, sem).wait()

    def near(body):
        for off in (0, 1, 2, nz - 2, nz - 1):
            body(lax.rem(z + off, nz))

    def far(body):
        for off in range(3, nz - 2):
            body(lax.rem(z + off, nz))

    def every(body):
        for o in range(nz):
            body(o)

    def states(j, some):
        def one(o):
            h = nz * j + o
            c = columns_of(h)
            kf = feature(k_ref[:, c].astype(F32)).astype(BF16)
            kf_buf[h] = kf
            s_out[0, j, o] = dot_tn(kf, v_ref[:, c]).astype(BF16)

        some(one)

    def before(j):
        load(2, j).wait()
        load(3, j).wait()

        def one(o):
            h = nz * j + o
            c = columns_of(h)
            qf = feature(q_ref[:, c].astype(F32)).astype(BF16)
            qf_buf[h] = qf
            a_buf[h] = jnp.where(causal, dot_nt(qf, kf_buf[h]), 0.0).astype(BF16)

        every(one)

    averaging = jnp.full((HD, HD), 1.0 / HD, BF16)

    def row_mean(product):
        return dot_nn(product.astype(BF16), averaging)

    def tag_of(message):
        return message[pl.ds(HD, TAG), :].astype(F32)[0:1, :]

    def value_of(message):
        return message[pl.ds(0, HD), :].astype(F32)

    def put(message, value, tag):
        message[pl.ds(0, HD), :] = value.astype(BF16)
        message[pl.ds(HD, TAG), :] = jnp.broadcast_to(tag, (TAG, HD)).astype(BF16)

    def send_to(src, dst, way, phase, j, device):
        remote(src, dst, send_a.at[way, phase, j], recv_a.at[way, phase, j], device).start()

    def send_more_to(src, dst, way, phase, j, device):
        remote(
            src, dst, send_more.at[way, phase, j], recv_more.at[way, phase, j], device
        ).start()

    def one_more(way, phase, j, sem):
        part = aux_in.at[way, j, 0]
        pltpu.make_async_copy(part, part, sem.at[way, phase, j]).wait()

    def leans(j):
        return j % 2 == 1

    def split_at(j, v):
        return (v == nz - 1) | (v <= 1) if leans(j) else (v >= nz - 2) | (v == 0)

    def split_for(j, v):
        return (v == 2) | (v == 3) | (v == 5) if leans(j) else (v == 2) | (v == 4) | (v == 5)

    def spread(way, j):
        v = place(way)
        source = s_out.at[way, j]
        into = leaf_in.at[way, j]
        beyond = line(way, v + 2 if leans(j) else v - 2)
        send_to(source.at[slot(v - 4)], into.at[1], way, 0, j, beyond)
        send_to(source.at[slot(v - 3)], into.at[0], way, 0, j, line(way, v - 1))
        send_to(source.at[slot(v + 3)], into.at[2], way, 0, j, line(way, v + 1))

    def collect(way, j):
        v = place(way)
        alone = alike(doc_at(way, v), following(way, v))
        mine, up, into = s_out.at[way, j], up_out.at[way, j], up_in.at[way, j]

        def state(u):
            return mine[slot(u)].astype(F32)

        up[0] = (alone * state(v - 1)).astype(BF16)
        up[1] = (alone * state(v + 1)).astype(BF16)
        into[v] = (alone * state(v)).astype(BF16)
        send_to(up.at[0], into.at[v], way, 1, j, line(way, v - 1))
        send_to(up.at[1], into.at[v], way, 1, j, line(way, v + 1))
        wait_in(leaf_in.at[way, j], recv_a.at[way, 0, j], 3)
        first, second, behind = (leaf_in[way, j, i].astype(F32) for i in range(3))
        ahead, back = (1, 2) if leans(j) else (2, 1)
        after_run = following(way, jnp.minimum(v + ahead, nz - 1))

        def weight(inside, u, target):
            return inside.astype(F32) * alike(doc_at(way, u), target)

        forward = (
            alike(doc_at(way, v), after_run) * state(v - 2)
            + weight(v + 1 < nz, v + 1, after_run) * first
        )
        if not leans(j):
            forward = forward + weight(v + 2 < nz, v + 2, after_run) * second
        up[2] = forward.astype(BF16)
        send_to(up.at[2], into.at[v], way, 1, j, line(way, v - 2))
        backward = alone * state(v + 2) + weight(v > 0, v - 1, following(way, v)) * behind
        if leans(j):
            backward = backward + weight(v > 1, v - 2, following(way, v)) * second
        up[3] = backward.astype(BF16)
        send_to(up.at[3], into.at[jnp.maximum(v - back, 0)], way, 1, j, line(way, v + 2))

        @pl.when(v >= nz - ahead)
        def _():
            target = doc_at(way, v + 1 + ahead)
            rest = weight(v + 1 >= nz, v + 1, target) * first
            if not leans(j):
                rest = rest + weight(v + 2 >= nz, v + 2, target) * second
            up[4] = rest.astype(BF16)
            send_more_to(up.at[4], into.at[0], way, 0, j, line(way, v - 2))

        @pl.when(v < back)
        def _():
            target = doc_at(way, nz - 1)
            rest = weight(v < 1, v - 1, target) * behind
            if leans(j):
                rest = rest + weight(v < 2, v - 2, target) * second
            up[4] = rest.astype(BF16)
            send_more_to(up.at[4], into.at[slot(v - back)], way, 0, j, line(way, v + 2))

    def segments(way, j):
        v = place(way)
        result = []
        for i in range(nz):
            off = lax.rem(i - v + nz, nz)
            if leans(j):
                length = jnp.where(off == 2, 2, jnp.where(off == 4, 3, 1))
                inner = (off == 3) | (off == 5) | (off == 6)
                cut = 5
            else:
                length = jnp.where(off == 2, 3, jnp.where(off == 5, 2, 1))
                inner = (off == 3) | (off == 4) | (off == 6)
                cut = 3
            if i == 0:
                length = jnp.where(off == cut, 2, length)
                start = None
                keep = alike(doc_at(way, i), following(way, i + length - 1))
            else:
                start = jnp.logical_not(inner)
                end = jnp.minimum(i + length - 1, nz - 1)
                keep = jnp.where(inner, 1.0, alike(doc_at(way, i), following(way, end)))
            result.append((start, keep))
        return result

    def part_of(way, j, i, start):
        value = up_in[way, j, i].astype(F32)
        return value if start is None else jnp.where(start, value, 0.0)

    def group_sum(way, j):
        v = place(way)
        wait_in(up_in.at[way, j], recv_a.at[way, 1, j], 4)

        @pl.when(split_for(j, v))
        def _():
            one_more(way, 0, j, recv_more)

        total = jnp.zeros((HD, HD), F32)
        for i, (start, keep) in enumerate(segments(way, j)):
            total = keep * total + part_of(way, j, i, start)
        edge = doc_at(way, nz - 1)
        put(g_out.at[way, j], total, edge.astype(F32) * jnp.ones((1, HD), F32))
        remote(
            g_out.at[way, j], g_in.at[way, j], send_g.at[way, j], recv_g.at[way, j], peer
        ).start()

    def chip_sum(way, j):
        pltpu.make_async_copy(g_in.at[way, j], g_in.at[way, j], recv_g.at[way, j]).wait()
        mine, other = g_out.at[way, j], g_in.at[way, j]
        late = core_one if way == 0 else 1.0 - core_one
        same = alike(tag_of(mine), tag_of(other))
        keep_mine = late + (1.0 - late) * same
        keep_other = (1.0 - late) + late * same
        put(
            t_out.at[way, j],
            keep_mine * value_of(mine) + keep_other * value_of(other),
            late * tag_of(mine) + (1.0 - late) * tag_of(other),
        )
        for d, device in enumerate(rows):
            remote(
                t_out.at[way, j],
                t_in.at[way, j, d],
                send_t.at[way, j],
                recv_t.at[way, j],
                device,
            ).start()

    def row_sum(way, j):
        if nx > 1:
            wait_in(t_in.at[way, j], recv_t.at[way, j], nx - 1)
        edge = nx - 1 if way == 0 else 0
        parts = [(t_out.at[way, j], x)] + [
            (t_in.at[way, j, d], lax.rem(x + nx - 1 - d, nx)) for d in range(nx - 1)
        ]
        tag = jnp.zeros((1, HD), F32)
        for part, place in parts:
            tag = tag + alike(place, edge) * tag_of(part)
        total = jnp.zeros((HD, HD), F32)
        for part, place in parts:
            total = total + alike(tag_of(part), tag) * value_of(part)
        put(u_out.at[way, j], total, tag)
        for d, device in enumerate(columns):
            remote(
                u_out.at[way, j],
                u_in.at[way, j, d],
                send_u.at[way, j],
                recv_u.at[way, j],
                device,
            ).start()

    def hand_back(way, j):
        if ny > 1:
            wait_in(u_in.at[way, j], recv_u.at[way, j], ny - 1)
        want = (doc[0] if way == 0 else doc[nz - 1]).astype(F32)
        late = core_one if way == 0 else 1.0 - core_one
        other = g_in.at[way, j]
        running = late * alike(tag_of(other), want) * value_of(other)
        for d in range(nx - 1):
            before_me = (x >= d + 1) if way == 0 else (x < d + 1)
            part = t_in.at[way, j, d]
            running = running + before_me.astype(F32) * alike(tag_of(part), want) * value_of(part)
        for d in range(ny - 1):
            before_me = (y >= d + 1) if way == 0 else (y < d + 1)
            part = u_in.at[way, j, d]
            running = running + before_me.astype(F32) * alike(tag_of(part), want) * value_of(part)
        v = place(way)
        for i, (start, keep) in enumerate(segments(way, j)):
            p_out[way, j, i] = running.astype(BF16)
            if i < nz - 1:
                running = keep * running + part_of(way, j, i, start)
        out, into, aux = p_out.at[way, j], p_in.at[way, j], aux_in.at[way, j]
        ahead, back = (1, 2) if leans(j) else (2, 1)
        behind = slot(v - 2)
        begin = jnp.maximum(behind - back, 0)
        send_to(out.at[begin], aux.at[0], way, 2, j, line(way, v - 2))
        send_to(out.at[slot(v + 2)], into.at[v], way, 2, j, line(way, v + 2))

        @pl.when(slot(v + 2) >= nz - ahead)
        def _():
            send_more_to(out.at[0], aux.at[1], way, 1, j, line(way, v + 2))

        @pl.when(behind < back)
        def _():
            send_more_to(out.at[slot(behind - back)], aux.at[1], way, 1, j, line(way, v - 2))

        send_to(out.at[slot(v - 1)], into.at[v], way, 2, j, line(way, v - 1))
        send_to(out.at[slot(v + 1)], into.at[v], way, 2, j, line(way, v + 1))
        p_in[way, j, v] = p_out[way, j, v]

    def expand(way, j):
        v = place(way)
        wait_in(p_in.at[way, j], recv_a.at[way, 2, j], 4)
        more = split_at(j, v)

        @pl.when(more)
        def _():
            one_more(way, 1, j, recv_more)

        mine, leaf = s_out.at[way, j], leaf_in.at[way, j]
        aux, out = aux_in.at[way, j], ex_out.at[way, j]
        ours, theirs = p_in.at[way, j, slot(v - 2)], p_in.at[way, j, slot(v + 2)]

        def step(u, value, state):
            return alike(doc_at(way, u), doc_at(way, u + 1)) * (value + state.astype(F32))

        extra = jnp.where(more, aux[1].astype(F32), 0.0)
        begin = aux[0].astype(F32)
        one = jnp.where(v + 1 == nz, extra, step(v, ours[...].astype(F32), mine[slot(v - 2)]))
        if leans(j):
            far_one = jnp.where(v < 2, extra, begin)
            out[1] = far_one.astype(BF16)
            send_to(out.at[1], theirs, way, 3, j, line(way, v - 2))
            last_one = jnp.where(v == 1, begin, step(v - 2, far_one, leaf[1]))
        else:
            far_one = jnp.where(v + 2 == nz, extra, step(v + 1, one, leaf[0]))
            out[1] = far_one.astype(BF16)
            send_to(out.at[1], ours, way, 3, j, line(way, v + 2))
            last_one = jnp.where(v == 0, extra, begin)
        out[0] = one.astype(BF16)
        send_to(out.at[0], ours, way, 3, j, line(way, v + 1))
        out[2] = last_one.astype(BF16)
        send_to(out.at[2], theirs, way, 3, j, line(way, v - 1))
        here = jnp.where(v == 0, begin, step(v - 1, last_one, leaf[2]))
        theirs[...] = here.astype(BF16)

    def middle(j, some):
        def one(o):
            h = nz * j + o
            c = columns_of(h)
            qf = qf_buf[h]
            raw = dot_nn(a_buf[h], v_ref[:, c]) + dot_nn(qf, p_in[0, j, o])
            inverse = lax.rsqrt(row_mean(raw * raw) + 1e-06)
            normed = raw * inverse
            att_ref[:, c] = normed.astype(BF16)
            wide = g_ref[:, c].astype(F32)
            along = row_mean(wide * normed)
            scaled = ((wide - normed * along) * inverse).astype(BF16)
            sc_buf[h] = scaled
            s_out[1, j, nz - 1 - o] = dot_tn(qf, scaled).astype(BF16)

        some(one)

    def middle_far(j):
        wait_in(p_in.at[0, j], recv_a.at[0, 3, j], 3)
        middle(j, far)
        spread(1, j)

    def after(j):
        def one(o):
            h = nz * j + o
            c = columns_of(h)
            scaled = sc_buf[h]
            mixed = jnp.where(causal, dot_nt(scaled, v_ref[:, c]), 0.0).astype(BF16)
            grad = dot_nn(mixed, kf_buf[h]) + dot_nt(scaled, p_in[0, j, o])
            qg_ref[:, c] = (grad * slope(q_ref[:, c].astype(F32))).astype(BF16)
            kl_buf[h] = dot_tn(mixed, qf_buf[h])
            vl_buf[h] = dot_tn(a_buf[h], scaled)

        every(one)

    def finish(j, some):
        def one(o):
            h = nz * j + o
            c = columns_of(h)
            state = p_in[1, j, nz - 1 - o]
            grad = kl_buf[h] + dot_nt(v_ref[:, c], state)
            kg_ref[:, c] = (grad * slope(k_ref[:, c].astype(F32))).astype(BF16)
            vg_ref[:, c] = (vl_buf[h] + dot_nn(kf_buf[h], state)).astype(BF16)

        some(one)

    def finish_far(j):
        wait_in(p_in.at[1, j], recv_a.at[1, 3, j], 3)
        finish(j, far)

    def start_states(j):
        load(0, j).wait()
        load(1, j).wait()
        states(j, far)
        if j == 0:
            pl.semaphore_wait(barrier, len(everyone))
        spread(0, j)

    steps = {
        "S": start_states,
        "B": before,
        "T": lambda j: states(j, near),
        "N": lambda j: middle(j, near),
        "M": middle_far,
        "A": after,
        "O": lambda j: finish(j, near),
        "F": finish_far,
        "C": functools.partial(collect, 0),
        "E": functools.partial(expand, 0),
        "c": functools.partial(collect, 1),
        "e": functools.partial(expand, 1),
        "G": functools.partial(group_sum, 0),
        "X": functools.partial(chip_sum, 0),
        "Y": functools.partial(row_sum, 0),
        "H": functools.partial(hand_back, 0),
        "g": functools.partial(group_sum, 1),
        "x": functools.partial(chip_sum, 1),
        "y": functools.partial(row_sum, 1),
        "h": functools.partial(hand_back, 1),
    }
    for step in plan(chunks):
        steps[step[0]](int(step[1:]))

    for way in range(2):
        v = place(way)
        for j in range(chunks):
            for phase, count in enumerate((3, 4, 4, 3)):
                wait_in(p_in.at[way, j], send_a.at[way, phase, j], count)
            pltpu.make_async_copy(g_in.at[way, j], g_in.at[way, j], send_g.at[way, j]).wait()
            if nx > 1:
                wait_in(t_in.at[way, j], send_t.at[way, j], nx - 1)
            if ny > 1:
                wait_in(u_in.at[way, j], send_u.at[way, j], ny - 1)

            @pl.when(split_at(j, v))
            def _():
                one_more(way, 0, j, send_more)

            @pl.when(split_for(j, v))
            def _():
                one_more(way, 1, j, send_more)


def shards(ny, nx, queries, key_vectors, value_vectors, out_grad, doc_ids):
    nz = lax.axis_size("head")
    tokens, features = queries.shape
    count = features // HD
    chunks = count // nz
    anywhere = pl.BlockSpec(memory_space=pl.ANY)
    half = functools.partial(pltpu.VMEM, dtype=BF16)
    wide = functools.partial(pltpu.VMEM, dtype=F32)
    dma = pltpu.SemaphoreType.DMA
    message = (HD + TAG, HD)
    out = pltpu.VMEM((tokens, features), BF16)
    return pl.pallas_call(
        functools.partial(kernel, ny, nx, nz, chunks),
        out_shape=(out,) * 4,
        in_specs=[pl.BlockSpec(memory_space=pltpu.SMEM)] + [anywhere] * 4,
        out_specs=(pl.BlockSpec(memory_space=pltpu.VMEM),) * 4,
        scratch_shapes=[half((tokens, features))] * 4
        + [dma((4, chunks))]
        + [
            half((count, HD, HD)),
            half((count, HD, HD)),
            half((count, HD, HD)),
            half((count, HD, HD)),
            wide((count, HD, HD)),
            wide((count, HD, HD)),
            half((2, chunks, nz, HD, HD)),
            half((2, chunks, 3, HD, HD)),
            half((2, chunks, 5, HD, HD)),
            half((2, chunks, nz, HD, HD)),
            half((2, chunks, nz, HD, HD)),
            half((2, chunks, nz, HD, HD)),
            half((2, chunks, 2, HD, HD)),
            half((2, chunks, 3, HD, HD)),
            half((2, chunks, *message)),
            half((2, chunks, *message)),
            half((2, chunks, *message)),
            half((2, chunks, max(nx - 1, 1), *message)),
            half((2, chunks, *message)),
            half((2, chunks, max(ny - 1, 1), *message)),
            dma((2, 4, chunks)),
            dma((2, 4, chunks)),
            dma((2, 2, chunks)),
            dma((2, 2, chunks)),
            dma((2, chunks)),
            dma((2, chunks)),
            dma((2, chunks)),
            dma((2, chunks)),
            dma((2, chunks)),
            dma((2, chunks)),
        ],
        compiler_params=pltpu.CompilerParams(
            collective_id=0, has_side_effects=True, vmem_limit_bytes=56 * 2**20
        ),
    )(doc_ids, queries, key_vectors, value_vectors, out_grad)


def build(mesh, ny, nx):
    spec = P(("ctx", "head"), None)
    return jax.shard_map(
        functools.partial(shards, ny, nx),
        mesh=mesh,
        in_specs=(spec,) * 4 + (P("ctx"),),
        out_specs=(spec,) * 4,
        check_vma=False,
    )


def solution(mesh):
    return build(mesh, 4, 4)
```

```python
import functools

import jax
import jax.numpy as jnp
from jax import lax
from jax.experimental import pallas as pl
from jax.experimental.pallas import tpu as pltpu
from jax.sharding import PartitionSpec as P

HD = 128
TAG = 16
MESH = pl.DeviceIdType.MESH
F32 = jnp.float32
BF16 = jnp.bfloat16


def feature(x):
    return jnp.where(x > 0, x + 1.0, jnp.exp(jnp.minimum(x, 0.0)))


def slope(x):
    return jnp.where(x > 0, jnp.ones_like(x), jnp.exp(jnp.minimum(x, 0.0)))


def dot_nn(a, b):
    return lax.dot_general(a, b, (((1,), (0,)), ((), ())), preferred_element_type=F32)


def dot_nt(a, b):
    return lax.dot_general(a, b, (((1,), (1,)), ((), ())), preferred_element_type=F32)


def dot_tn(a, b):
    return lax.dot_general(a, b, (((0,), (0,)), ((), ())), preferred_element_type=F32)


def plan(chunks):
    if chunks == 4:
        order = [
            "S0 S1 T0 T1",
            "B0 B1 S3 S2",
            "C1 T3 T2 B2",
            "C0 G1 C2 X1",
            "C3 G0 B3 X0",
            "Y1 G2 Y0 X2",
            "H1 G3 X3 Y2",
            "H0 E1 Y3 H2",
            "N1 E0 H3 N0",
            "M1 E2 M0 E3",
            "c1 M2 c0 N2",
            "M3 N3 g1 c2",
            "A1 x1 g0 c3",
            "x0 g2 y1 x2",
            "g3 y0 x3 h1",
            "y2 h0 y3 h2",
            "A3 h3 A0 e0",
            "e2 e1 e3 A2",
            "O0 F0 O3 O1",
            "F1 O2 F2 F3",
        ]
        return " ".join(order).split()
    return [f"{step}{j}" for step in "STBCGXYHENMAcgxyheOF" for j in range(chunks)]


def kernel(
    ny,
    nx,
    nz,
    chunks,
    ids,
    q_hbm,
    k_hbm,
    v_hbm,
    g_hbm,
    att_ref,
    qg_ref,
    kg_ref,
    vg_ref,
    q_ref,
    k_ref,
    v_ref,
    g_ref,
    load_sem,
    kf_buf,
    qf_buf,
    a_buf,
    sc_buf,
    kl_buf,
    vl_buf,
    s_out,
    leaf_in,
    up_out,
    up_in,
    p_out,
    p_in,
    aux_in,
    ex_out,
    g_out,
    g_in,
    t_out,
    t_in,
    u_out,
    u_in,
    send_a,
    recv_a,
    send_more,
    recv_more,
    send_g,
    recv_g,
    send_t,
    recv_t,
    send_u,
    recv_u,
):
    ctx = lax.axis_index("ctx")
    z = lax.axis_index("head")
    core = lax.rem(ctx, 2)
    x = lax.rem(ctx // 2, nx)
    y = ctx // (2 * nx)

    def at(yy, xx, cc):
        return (yy * nx + xx) * 2 + cc

    peer = (at(y, x, 1 - core), z)
    lines = [(ctx, lax.rem(z + d, nz)) for d in (1, 2, nz - 1, nz - 2)]
    rows = [(at(y, lax.rem(x + d, nx), core), z) for d in range(1, nx)]
    columns = [(at(lax.rem(y + d, ny), x, core), z) for d in range(1, ny)]
    everyone = lines + rows + columns + [peer]

    barrier = pltpu.get_barrier_semaphore()
    for device in everyone:
        pl.semaphore_signal(barrier, inc=1, device_id=device, device_id_type=MESH)

    def block(ref, j):
        return ref.at[:, pl.ds(j * nz * HD, nz * HD)]

    def load(i, j):
        hbm, ref = ((k_hbm, k_ref), (v_hbm, v_ref), (q_hbm, q_ref), (g_hbm, g_ref))[i]
        return pltpu.make_async_copy(block(hbm, j), block(ref, j), load_sem.at[i, j])

    for i in range(0, 4, 2):
        for j in range(chunks):
            load(i, j).start()
            load(i + 1, j).start()

    core_one = (core == 1).astype(F32)
    doc = [ids[i] for i in range(nz)]
    causal = lax.broadcasted_iota(jnp.int32, (HD, HD), 0) >= lax.broadcasted_iota(
        jnp.int32, (HD, HD), 1
    )

    def alike(a, b):
        return jnp.where(a == b, 1.0, 0.0).astype(F32)

    def place(way):
        return z if way == 0 else nz - 1 - z

    def line(way, v):
        v = lax.rem(v + 2 * nz, nz)
        return (ctx, v if way == 0 else nz - 1 - v)

    def doc_at(way, v):
        v = lax.rem(v + 2 * nz, nz)
        return ids[v if way == 0 else nz - 1 - v]

    def following(way, v):
        return doc_at(way, jnp.minimum(v + 1, nz - 1))

    def slot(v):
        return lax.rem(v + 2 * nz, nz)

    def head_slot(way, o):
        return o if way == 0 else nz - 1 - o

    def columns_of(h):
        return pl.ds(pl.multiple_of(h * HD, HD), HD)

    def remote(src, dst, send, recv, device):
        return pltpu.make_async_remote_copy(
            src_ref=src,
            dst_ref=dst,
            send_sem=send,
            recv_sem=recv,
            device_id=device,
            device_id_type=MESH,
        )

    def wait_in(into, sem, count):
        part = into.at[pl.ds(0, count)]
        pltpu.make_async_copy(part, part, sem).wait()

    def near(body):
        for off in (0, 1, 2, nz - 2, nz - 1):
            body(lax.rem(z + off, nz))

    def far(body):
        for off in range(3, nz - 2):
            body(lax.rem(z + off, nz))

    def every(body):
        for o in range(nz):
            body(o)

    def states(j, some):
        def one(o):
            h = nz * j + o
            c = columns_of(h)
            kf = feature(k_ref[:, c].astype(F32)).astype(BF16)
            kf_buf[h] = kf
            s_out[0, j, o] = dot_tn(kf, v_ref[:, c]).astype(BF16)

        some(one)

    def before(j):
        load(2, j).wait()
        load(3, j).wait()

        def one(o):
            h = nz * j + o
            c = columns_of(h)
            qf = feature(q_ref[:, c].astype(F32)).astype(BF16)
            qf_buf[h] = qf
            a_buf[h] = jnp.where(causal, dot_nt(qf, kf_buf[h]), 0.0).astype(BF16)

        every(one)

    averaging = jnp.full((HD, HD), 1.0 / HD, BF16)

    def row_mean(product):
        return dot_nn(product.astype(BF16), averaging)

    def tag_of(message):
        return message[pl.ds(HD, TAG), :].astype(F32)[0:1, :]

    def value_of(message):
        return message[pl.ds(0, HD), :].astype(F32)

    def put(message, value, tag):
        message[pl.ds(0, HD), :] = value.astype(BF16)
        message[pl.ds(HD, TAG), :] = jnp.broadcast_to(tag, (TAG, HD)).astype(BF16)

    def send_to(src, dst, way, phase, j, device):
        remote(src, dst, send_a.at[way, phase, j], recv_a.at[way, phase, j], device).start()

    def send_more_to(src, dst, way, phase, j, device):
        remote(
            src, dst, send_more.at[way, phase, j], recv_more.at[way, phase, j], device
        ).start()

    def one_more(way, phase, j, sem):
        part = aux_in.at[way, j, 0]
        pltpu.make_async_copy(part, part, sem.at[way, phase, j]).wait()

    def leans(j):
        return j % 2 == 1

    def split_at(j, v):
        return (v == nz - 1) | (v <= 1) if leans(j) else (v >= nz - 2) | (v == 0)

    def split_for(j, v):
        return (v == 2) | (v == 3) | (v == 5) if leans(j) else (v == 2) | (v == 4) | (v == 5)

    def spread(way, j):
        v = place(way)
        source = s_out.at[way, j]
        into = leaf_in.at[way, j]
        beyond = line(way, v + 2 if leans(j) else v - 2)
        send_to(source.at[slot(v - 4)], into.at[1], way, 0, j, beyond)
        send_to(source.at[slot(v - 3)], into.at[0], way, 0, j, line(way, v - 1))
        send_to(source.at[slot(v + 3)], into.at[2], way, 0, j, line(way, v + 1))

    def collect(way, j):
        v = place(way)
        alone = alike(doc_at(way, v), following(way, v))
        mine, up, into = s_out.at[way, j], up_out.at[way, j], up_in.at[way, j]

        def state(u):
            return mine[slot(u)].astype(F32)

        up[0] = (alone * state(v - 1)).astype(BF16)
        up[1] = (alone * state(v + 1)).astype(BF16)
        into[v] = (alone * state(v)).astype(BF16)
        send_to(up.at[0], into.at[v], way, 1, j, line(way, v - 1))
        send_to(up.at[1], into.at[v], way, 1, j, line(way, v + 1))
        wait_in(leaf_in.at[way, j], recv_a.at[way, 0, j], 3)
        first, second, behind = (leaf_in[way, j, i].astype(F32) for i in range(3))
        ahead, back = (1, 2) if leans(j) else (2, 1)
        after_run = following(way, jnp.minimum(v + ahead, nz - 1))

        def weight(inside, u, target):
            return inside.astype(F32) * alike(doc_at(way, u), target)

        forward = (
            alike(doc_at(way, v), after_run) * state(v - 2)
            + weight(v + 1 < nz, v + 1, after_run) * first
        )
        if not leans(j):
            forward = forward + weight(v + 2 < nz, v + 2, after_run) * second
        up[2] = forward.astype(BF16)
        send_to(up.at[2], into.at[v], way, 1, j, line(way, v - 2))
        backward = alone * state(v + 2) + weight(v > 0, v - 1, following(way, v)) * behind
        if leans(j):
            backward = backward + weight(v > 1, v - 2, following(way, v)) * second
        up[3] = backward.astype(BF16)
        send_to(up.at[3], into.at[jnp.maximum(v - back, 0)], way, 1, j, line(way, v + 2))

        @pl.when(v >= nz - ahead)
        def _():
            target = doc_at(way, v + 1 + ahead)
            rest = weight(v + 1 >= nz, v + 1, target) * first
            if not leans(j):
                rest = rest + weight(v + 2 >= nz, v + 2, target) * second
            up[4] = rest.astype(BF16)
            send_more_to(up.at[4], into.at[0], way, 0, j, line(way, v - 2))

        @pl.when(v < back)
        def _():
            target = doc_at(way, nz - 1)
            rest = weight(v < 1, v - 1, target) * behind
            if leans(j):
                rest = rest + weight(v < 2, v - 2, target) * second
            up[4] = rest.astype(BF16)
            send_more_to(up.at[4], into.at[slot(v - back)], way, 0, j, line(way, v + 2))

    def segments(way, j):
        v = place(way)
        result = []
        for i in range(nz):
            off = lax.rem(i - v + nz, nz)
            if leans(j):
                length = jnp.where(off == 2, 2, jnp.where(off == 4, 3, 1))
                inner = (off == 3) | (off == 5) | (off == 6)
                cut = 5
            else:
                length = jnp.where(off == 2, 3, jnp.where(off == 5, 2, 1))
                inner = (off == 3) | (off == 4) | (off == 6)
                cut = 3
            if i == 0:
                length = jnp.where(off == cut, 2, length)
                start = None
                keep = alike(doc_at(way, i), following(way, i + length - 1))
            else:
                start = jnp.logical_not(inner)
                end = jnp.minimum(i + length - 1, nz - 1)
                keep = jnp.where(inner, 1.0, alike(doc_at(way, i), following(way, end)))
            result.append((start, keep))
        return result

    def part_of(way, j, i, start):
        value = up_in[way, j, i].astype(F32)
        return value if start is None else jnp.where(start, value, 0.0)

    def group_sum(way, j):
        v = place(way)
        wait_in(up_in.at[way, j], recv_a.at[way, 1, j], 4)

        @pl.when(split_for(j, v))
        def _():
            one_more(way, 0, j, recv_more)

        total = jnp.zeros((HD, HD), F32)
        for i, (start, keep) in enumerate(segments(way, j)):
            total = keep * total + part_of(way, j, i, start)
        edge = doc_at(way, nz - 1)
        put(g_out.at[way, j], total, edge.astype(F32) * jnp.ones((1, HD), F32))
        remote(
            g_out.at[way, j], g_in.at[way, j], send_g.at[way, j], recv_g.at[way, j], peer
        ).start()

    def chip_sum(way, j):
        pltpu.make_async_copy(g_in.at[way, j], g_in.at[way, j], recv_g.at[way, j]).wait()
        mine, other = g_out.at[way, j], g_in.at[way, j]
        late = core_one if way == 0 else 1.0 - core_one
        same = alike(tag_of(mine), tag_of(other))
        keep_mine = late + (1.0 - late) * same
        keep_other = (1.0 - late) + late * same
        put(
            t_out.at[way, j],
            keep_mine * value_of(mine) + keep_other * value_of(other),
            late * tag_of(mine) + (1.0 - late) * tag_of(other),
        )
        for d, device in enumerate(rows):
            remote(
                t_out.at[way, j],
                t_in.at[way, j, d],
                send_t.at[way, j],
                recv_t.at[way, j],
                device,
            ).start()

    def row_sum(way, j):
        if nx > 1:
            wait_in(t_in.at[way, j], recv_t.at[way, j], nx - 1)
        edge = nx - 1 if way == 0 else 0
        parts = [(t_out.at[way, j], x)] + [
            (t_in.at[way, j, d], lax.rem(x + nx - 1 - d, nx)) for d in range(nx - 1)
        ]
        tag = jnp.zeros((1, HD), F32)
        for part, place in parts:
            tag = tag + alike(place, edge) * tag_of(part)
        total = jnp.zeros((HD, HD), F32)
        for part, place in parts:
            total = total + alike(tag_of(part), tag) * value_of(part)
        put(u_out.at[way, j], total, tag)
        for d, device in enumerate(columns):
            remote(
                u_out.at[way, j],
                u_in.at[way, j, d],
                send_u.at[way, j],
                recv_u.at[way, j],
                device,
            ).start()

    def hand_back(way, j):
        if ny > 1:
            wait_in(u_in.at[way, j], recv_u.at[way, j], ny - 1)
        want = (doc[0] if way == 0 else doc[nz - 1]).astype(F32)
        late = core_one if way == 0 else 1.0 - core_one
        other = g_in.at[way, j]
        running = late * alike(tag_of(other), want) * value_of(other)
        for d in range(nx - 1):
            before_me = (x >= d + 1) if way == 0 else (x < d + 1)
            part = t_in.at[way, j, d]
            running = running + before_me.astype(F32) * alike(tag_of(part), want) * value_of(part)
        for d in range(ny - 1):
            before_me = (y >= d + 1) if way == 0 else (y < d + 1)
            part = u_in.at[way, j, d]
            running = running + before_me.astype(F32) * alike(tag_of(part), want) * value_of(part)
        v = place(way)
        for i, (start, keep) in enumerate(segments(way, j)):
            p_out[way, j, i] = running.astype(BF16)
            if i < nz - 1:
                running = keep * running + part_of(way, j, i, start)
        out, into, aux = p_out.at[way, j], p_in.at[way, j], aux_in.at[way, j]
        ahead, back = (1, 2) if leans(j) else (2, 1)
        behind = slot(v - 2)
        begin = jnp.maximum(behind - back, 0)
        send_to(out.at[begin], aux.at[0], way, 2, j, line(way, v - 2))
        send_to(out.at[slot(v + 2)], into.at[v], way, 2, j, line(way, v + 2))

        @pl.when(slot(v + 2) >= nz - ahead)
        def _():
            send_more_to(out.at[0], aux.at[1], way, 1, j, line(way, v + 2))

        @pl.when(behind < back)
        def _():
            send_more_to(out.at[slot(behind - back)], aux.at[1], way, 1, j, line(way, v - 2))

        send_to(out.at[slot(v - 1)], into.at[v], way, 2, j, line(way, v - 1))
        send_to(out.at[slot(v + 1)], into.at[v], way, 2, j, line(way, v + 1))
        p_in[way, j, v] = p_out[way, j, v]

    def expand(way, j):
        v = place(way)
        wait_in(p_in.at[way, j], recv_a.at[way, 2, j], 4)
        more = split_at(j, v)

        @pl.when(more)
        def _():
            one_more(way, 1, j, recv_more)

        mine, leaf = s_out.at[way, j], leaf_in.at[way, j]
        aux, out = aux_in.at[way, j], ex_out.at[way, j]
        ours, theirs = p_in.at[way, j, slot(v - 2)], p_in.at[way, j, slot(v + 2)]

        def step(u, value, state):
            return alike(doc_at(way, u), doc_at(way, u + 1)) * (value + state.astype(F32))

        extra = jnp.where(more, aux[1].astype(F32), 0.0)
        begin = aux[0].astype(F32)
        one = jnp.where(v + 1 == nz, extra, step(v, ours[...].astype(F32), mine[slot(v - 2)]))
        if leans(j):
            far_one = jnp.where(v < 2, extra, begin)
            out[1] = far_one.astype(BF16)
            send_to(out.at[1], theirs, way, 3, j, line(way, v - 2))
            last_one = jnp.where(v == 1, begin, step(v - 2, far_one, leaf[1]))
        else:
            far_one = jnp.where(v + 2 == nz, extra, step(v + 1, one, leaf[0]))
            out[1] = far_one.astype(BF16)
            send_to(out.at[1], ours, way, 3, j, line(way, v + 2))
            last_one = jnp.where(v == 0, extra, begin)
        out[0] = one.astype(BF16)
        send_to(out.at[0], ours, way, 3, j, line(way, v + 1))
        out[2] = last_one.astype(BF16)
        send_to(out.at[2], theirs, way, 3, j, line(way, v - 1))
        here = jnp.where(v == 0, begin, step(v - 1, last_one, leaf[2]))
        theirs[...] = here.astype(BF16)

    def middle(j, some):
        def one(o):
            h = nz * j + o
            c = columns_of(h)
            qf = qf_buf[h]
            raw = dot_nn(a_buf[h], v_ref[:, c]) + dot_nn(qf, p_in[0, j, o])
            inverse = lax.rsqrt(row_mean(raw * raw) + 1e-06)
            normed = raw * inverse
            att_ref[:, c] = normed.astype(BF16)
            wide = g_ref[:, c].astype(F32)
            along = row_mean(wide * normed)
            scaled = ((wide - normed * along) * inverse).astype(BF16)
            sc_buf[h] = scaled
            s_out[1, j, nz - 1 - o] = dot_tn(qf, scaled).astype(BF16)

        some(one)

    def middle_far(j):
        wait_in(p_in.at[0, j], recv_a.at[0, 3, j], 3)
        middle(j, far)
        spread(1, j)

    def after(j):
        def one(o):
            h = nz * j + o
            c = columns_of(h)
            scaled = sc_buf[h]
            mixed = jnp.where(causal, dot_nt(scaled, v_ref[:, c]), 0.0).astype(BF16)
            grad = dot_nn(mixed, kf_buf[h]) + dot_nt(scaled, p_in[0, j, o])
            qg_ref[:, c] = (grad * slope(q_ref[:, c].astype(F32))).astype(BF16)
            kl_buf[h] = dot_tn(mixed, qf_buf[h])
            vl_buf[h] = dot_tn(a_buf[h], scaled)

        every(one)

    def finish(j, some):
        def one(o):
            h = nz * j + o
            c = columns_of(h)
            state = p_in[1, j, nz - 1 - o]
            grad = kl_buf[h] + dot_nt(v_ref[:, c], state)
            kg_ref[:, c] = (grad * slope(k_ref[:, c].astype(F32))).astype(BF16)
            vg_ref[:, c] = (vl_buf[h] + dot_nn(kf_buf[h], state)).astype(BF16)

        some(one)

    def finish_far(j):
        wait_in(p_in.at[1, j], recv_a.at[1, 3, j], 3)
        finish(j, far)

    def start_states(j):
        load(0, j).wait()
        load(1, j).wait()
        states(j, far)
        if j == 0:
            pl.semaphore_wait(barrier, len(everyone))
        spread(0, j)

    steps = {
        "S": start_states,
        "B": before,
        "T": lambda j: states(j, near),
        "N": lambda j: middle(j, near),
        "M": middle_far,
        "A": after,
        "O": lambda j: finish(j, near),
        "F": finish_far,
        "C": functools.partial(collect, 0),
        "E": functools.partial(expand, 0),
        "c": functools.partial(collect, 1),
        "e": functools.partial(expand, 1),
        "G": functools.partial(group_sum, 0),
        "X": functools.partial(chip_sum, 0),
        "Y": functools.partial(row_sum, 0),
        "H": functools.partial(hand_back, 0),
        "g": functools.partial(group_sum, 1),
        "x": functools.partial(chip_sum, 1),
        "y": functools.partial(row_sum, 1),
        "h": functools.partial(hand_back, 1),
    }
    for step in plan(chunks):
        steps[step[0]](int(step[1:]))

    for way in range(2):
        v = place(way)
        for j in range(chunks):
            for phase, count in enumerate((3, 4, 4, 3)):
                wait_in(p_in.at[way, j], send_a.at[way, phase, j], count)
            pltpu.make_async_copy(g_in.at[way, j], g_in.at[way, j], send_g.at[way, j]).wait()
            if nx > 1:
                wait_in(t_in.at[way, j], send_t.at[way, j], nx - 1)
            if ny > 1:
                wait_in(u_in.at[way, j], send_u.at[way, j], ny - 1)

            @pl.when(split_at(j, v))
            def _():
                one_more(way, 0, j, send_more)

            @pl.when(split_for(j, v))
            def _():
                one_more(way, 1, j, send_more)


def shards(ny, nx, queries, key_vectors, value_vectors, out_grad, doc_ids):
    nz = lax.axis_size("head")
    tokens, features = queries.shape
    count = features // HD
    chunks = count // nz
    anywhere = pl.BlockSpec(memory_space=pl.ANY)
    half = functools.partial(pltpu.VMEM, dtype=BF16)
    wide = functools.partial(pltpu.VMEM, dtype=F32)
    dma = pltpu.SemaphoreType.DMA
    message = (HD + TAG, HD)
    out = pltpu.VMEM((tokens, features), BF16)
    return pl.pallas_call(
        functools.partial(kernel, ny, nx, nz, chunks),
        out_shape=(out,) * 4,
        in_specs=[pl.BlockSpec(memory_space=pltpu.SMEM)] + [anywhere] * 4,
        out_specs=(pl.BlockSpec(memory_space=pltpu.VMEM),) * 4,
        scratch_shapes=[half((tokens, features))] * 4
        + [dma((4, chunks))]
        + [
            half((count, HD, HD)),
            half((count, HD, HD)),
            half((count, HD, HD)),
            half((count, HD, HD)),
            wide((count, HD, HD)),
            wide((count, HD, HD)),
            half((2, chunks, nz, HD, HD)),
            half((2, chunks, 3, HD, HD)),
            half((2, chunks, 5, HD, HD)),
            half((2, chunks, nz, HD, HD)),
            half((2, chunks, nz, HD, HD)),
            half((2, chunks, nz, HD, HD)),
            half((2, chunks, 2, HD, HD)),
            half((2, chunks, 3, HD, HD)),
            half((2, chunks, *message)),
            half((2, chunks, *message)),
            half((2, chunks, *message)),
            half((2, chunks, max(nx - 1, 1), *message)),
            half((2, chunks, *message)),
            half((2, chunks, max(ny - 1, 1), *message)),
            dma((2, 4, chunks)),
            dma((2, 4, chunks)),
            dma((2, 2, chunks)),
            dma((2, 2, chunks)),
            dma((2, chunks)),
            dma((2, chunks)),
            dma((2, chunks)),
            dma((2, chunks)),
            dma((2, chunks)),
            dma((2, chunks)),
        ],
        compiler_params=pltpu.CompilerParams(
            collective_id=0, has_side_effects=True, vmem_limit_bytes=56 * 2**20
        ),
    )(doc_ids, queries, key_vectors, value_vectors, out_grad)


def build(mesh, ny, nx):
    spec = P(("ctx", "head"), None)
    return jax.shard_map(
        functools.partial(shards, ny, nx),
        mesh=mesh,
        in_specs=(spec,) * 4 + (P("ctx"),),
        out_specs=(spec,) * 4,
        check_vma=False,
    )


def solution(mesh):
    return build(mesh, 4, 4)
```
